32 devices in a mesh: rep: 2 (over core), fsdp: 16 (over z, y, x).
Axes of the slice: x: 2, y: 2, z: 4, core: 2. Of those that a mesh axis runs over, the one named last changes fastest.
Arguments:
- tokens: bfloat16 [4096, 8192], P('fsdp'), as said below
- query_ckpt: float32 [2, 8192, 1024], P('rep', 'fsdp'), as said below
- key_value_ckpt: float32 [2, 8192, 256], P('rep', 'fsdp'), as said below
- numerators: int32 [2], replicated, may hold values from 1 to 8
Outputs:
- context: bfloat16 [4096, 1024], P('fsdp')
The draws below stay inside these ranges and needn't reach their ends.
Inputs may be any that keep to these rules, and one draw needn't show every extreme that they name: `tokens`: hidden states of mixed scales. `query_ckpt`: checkpoint weights. `key_value_ckpt`: checkpoint weights.
All inputs are finite; a program needn't handle non-finite values.
Results may differ from the reference program's by a relative error of at most 0.0081.
Values may be sent and summed in bfloat16 or wider, within the bound.
A program may use at most 128 MiB of HBM per device.

```python
import math
import jax
import jax.numpy as jnp
from jax import lax

D = 8192
HEAD = 128
TOKENS = 4096
LENGTH = 4096
QW = 1024
KW = 128
N_REP = 2


def common_basis(key):
    basis_key = jax.random.fold_in(key, 77)
    return jax.random.normal(basis_key, (D, HEAD), jnp.float32) / math.sqrt(D)


def draw_query_ckpt(key, part):
    key = jax.random.fold_in(key, 1)
    base_key, noise_key = jax.random.split(key, 2)
    base_part = jax.random.normal(base_key, (D, QW), jnp.float32) * (0.5 / math.sqrt(D))
    noise_part = jax.random.normal(noise_key, (N_REP, D, QW), jnp.float32) * (0.5 / math.sqrt(D))
    return base_part[None] + noise_part


def draw_key_value_ckpt(key, part):
    key_basis = common_basis(key)
    key = jax.random.fold_in(key, 2)
    first_key, second_key, third_key = jax.random.split(key, 3)
    key_noise = jax.random.normal(first_key, (N_REP, D, KW), jnp.float32) * (0.6 / math.sqrt(D))
    value_base = jax.random.normal(second_key, (D, KW), jnp.float32) * (0.7 / math.sqrt(D))
    value_noise = jax.random.normal(third_key, (N_REP, D, KW), jnp.float32) * (0.7 / math.sqrt(D))
    key_part = key_basis[None] + key_noise
    value_part = value_base[None] + value_noise
    return jnp.concatenate([key_part, value_part], axis=2)


def draw_tokens(key, part):
    key = jax.random.fold_in(key, 3)
    first_key, second_key, third_key = jax.random.split(key, 3)
    raw_draw = jax.random.normal(first_key, (TOKENS, D), jnp.float32)
    row_scale = jnp.exp(jax.random.uniform(second_key, (TOKENS, 1), jnp.float32, math.log(0.3), math.log(3.0)))
    col_scale = jnp.exp(jax.random.uniform(third_key, (1, D), jnp.float32, math.log(0.3), math.log(3.0)))
    return (raw_draw * row_scale * col_scale).astype(jnp.bfloat16)


def setup_inputs(seed: int = 0) -> dict:
    key_of = jax.random.split(jax.random.key(seed), 5)
    return {
        "tokens": draw_tokens(jax.random.fold_in(key_of[4], 71), 0),
        "query_ckpt": draw_query_ckpt(jax.random.fold_in(key_of[4], 71), 0),
        "key_value_ckpt": draw_key_value_ckpt(jax.random.fold_in(key_of[4], 71), 0),
        "numerators": jax.random.randint(key_of[3], (N_REP,), 1, 9).astype(jnp.int32),
    }


theta_base = 500000.0
eps_norm = 1e-05
masked_score = -1e+30

def averaged(checkpoints, numerators):
    weight_sum = jnp.sum(numerators).astype(jnp.float32)
    shares = numerators.astype(jnp.float32) / weight_sum
    return lax.optimization_barrier(jnp.sum(shares[:, None, None] * checkpoints, axis=0)).astype(jnp.bfloat16)

def rms_normed(hidden):
    wide_copy = hidden.astype(jnp.float32)
    return (wide_copy * lax.rsqrt(lax.optimization_barrier(jnp.mean(wide_copy * wide_copy, axis=-1, keepdims=True)) + eps_norm)).astype(jnp.bfloat16)

def rotary(values, positions):
    half_size = values.shape[-1] // 2
    inverse_freq = jnp.exp(-(jnp.arange(half_size, dtype=jnp.float32) * (2.0 / values.shape[-1])) * math.log(theta_base))
    angles = positions.astype(jnp.float32)[:, None] * inverse_freq[None, :]
    cosine_table = jnp.cos(angles)[:, None, :]
    sine_table = jnp.sin(angles)[:, None, :]
    first_half = values[..., :half_size]
    second_half = values[..., half_size:]
    return jnp.concatenate([first_half * cosine_table - second_half * sine_table, second_half * cosine_table + first_half * sine_table], axis=-1)

def attend_heads(queries, pair_rows, query_pos, key_pos):
    head_size = queries.shape[-1]
    key_rows = pair_rows[:, :head_size]
    value_rows = pair_rows[:, head_size:]
    score_scale = 1.0 / math.sqrt(head_size)
    allowed = key_pos[None, :] <= query_pos[:, None]

    def one_head(query_head):
        scores = jnp.dot(query_head, key_rows.T, preferred_element_type=jnp.float32) * score_scale
        scores = jnp.where(allowed, scores, masked_score)
        row_top = lax.optimization_barrier(jnp.max(scores, axis=1, keepdims=True))
        weights_exp = jnp.exp(scores - row_top)
        norm_sum = lax.optimization_barrier(jnp.sum(weights_exp, axis=1, keepdims=True))
        mixed_out = jnp.dot(weights_exp.astype(jnp.bfloat16), value_rows, preferred_element_type=jnp.float32) / norm_sum
        return mixed_out.astype(jnp.bfloat16)
    head_outs = lax.map(one_head, jnp.transpose(queries, (1, 0, 2)))
    return jnp.transpose(head_outs, (1, 0, 2)).reshape(queries.shape[0], -1)

def project(normed, query_avg, pair_avg, positions):
    queries = jnp.dot(normed, query_avg, preferred_element_type=jnp.float32)
    pair_proj = jnp.dot(normed, pair_avg, preferred_element_type=jnp.float32)
    row_count = normed.shape[0]
    query_rot = rotary(queries.reshape(row_count, queries.shape[1] // HEAD, HEAD), positions).astype(jnp.bfloat16)
    key_rot = rotary(pair_proj[:, None, :HEAD], positions)[:, 0, :].astype(jnp.bfloat16)
    pair_rows = jnp.concatenate([key_rot, pair_proj[:, HEAD:].astype(jnp.bfloat16)], axis=1)
    return (query_rot, pair_rows)

def reference(tokens, query_ckpt, key_value_ckpt, numerators):
    query_avg = averaged(query_ckpt, numerators)
    pair_avg = averaged(key_value_ckpt, numerators)
    sequences = tokens.reshape(TOKENS // LENGTH, LENGTH, D)
    positions = jnp.arange(LENGTH, dtype=jnp.int32)

    def one_sequence(seq_tokens):
        normed = rms_normed(seq_tokens)
        query_rot, pair_rows = project(normed, query_avg, pair_avg, positions)
        return attend_heads(query_rot, pair_rows, positions, positions)
    outputs = lax.map(one_sequence, sequences)
    return outputs.reshape(TOKENS, -1)
```

```python
import math

import functools

import jax
import jax.numpy as jnp
from jax import lax
from jax.experimental import pallas as pl
from jax.experimental.pallas import tpu as pltpu
from jax.sharding import PartitionSpec as P

theta_base = 500000.0
eps_norm = 1e-05
masked_score = -1e30


def rms_normed(hidden):
    wide_copy = hidden.astype(jnp.float32)
    return (
        wide_copy * lax.rsqrt(jnp.mean(wide_copy * wide_copy, axis=-1, keepdims=True) + eps_norm)
    ).astype(jnp.bfloat16)


def rotary(values, positions):
    half_size = values.shape[-1] // 2
    inverse_freq = jnp.exp(
        -(jnp.arange(half_size, dtype=jnp.float32) * (2.0 / values.shape[-1]))
        * math.log(theta_base)
    )
    angles = positions.astype(jnp.float32)[:, None] * inverse_freq[None, :]
    cosine_table = jnp.cos(angles)[:, None, :]
    sine_table = jnp.sin(angles)[:, None, :]
    first_half = values[..., :half_size]
    second_half = values[..., half_size:]
    return jnp.concatenate(
        [
            first_half * cosine_table - second_half * sine_table,
            second_half * cosine_table + first_half * sine_table,
        ],
        axis=-1,
    )


def attend_heads(queries, pair_rows, query_pos, key_pos):
    head_size = queries.shape[-1]
    key_rows = pair_rows[:, :head_size]
    value_rows = pair_rows[:, head_size:]
    score_scale = 1.0 / math.sqrt(head_size)
    allowed = key_pos[None, :] <= query_pos[:, None]

    def one_head(query_head):
        scores = jnp.dot(query_head, key_rows.T, preferred_element_type=jnp.float32) * score_scale
        scores = jnp.where(allowed, scores, masked_score)
        row_top = jnp.max(scores, axis=1, keepdims=True)
        weights_exp = jnp.exp(scores - row_top)
        norm_sum = jnp.sum(weights_exp, axis=1, keepdims=True)
        mixed_out = (
            jnp.dot(
                weights_exp.astype(jnp.bfloat16), value_rows, preferred_element_type=jnp.float32
            )
            / norm_sum
        )
        return mixed_out.astype(jnp.bfloat16)

    head_outs = lax.map(one_head, jnp.transpose(queries, (1, 0, 2)))
    return jnp.transpose(head_outs, (1, 0, 2)).reshape(queries.shape[0], -1)


def local(tokens, query_ckpt, key_value_ckpt, numerators):
    fsdp_count = lax.axis_size("fsdp")
    rep_idx = lax.axis_index("rep")
    fsdp_idx = lax.axis_index("fsdp")
    slot_ids = jnp.arange(numerators.shape[0], dtype=jnp.int32)
    weight_sum = jnp.sum(numerators).astype(jnp.float32)
    my_share = (
        jnp.sum(jnp.where(slot_ids == rep_idx, numerators, 0)).astype(jnp.float32) / weight_sum
    )
    query_term = my_share * query_ckpt[0]
    pair_term = my_share * key_value_ckpt[0]
    tok_dev = tokens.shape[0]
    seq_length = tok_dev * fsdp_count
    offset = fsdp_idx * tok_dev
    normed = rms_normed(tokens)
    query_width = query_ckpt.shape[2]
    pair_width = key_value_ckpt.shape[2]
    query_sum, pair_sum = lax.psum((query_term, pair_term), "rep")
    query_rows = query_sum.astype(jnp.bfloat16)
    pair_rows = pair_sum.astype(jnp.bfloat16)
    queries = jnp.dot(
        normed,
        lax.all_gather(query_rows, "fsdp", axis=0, tiled=True),
        preferred_element_type=jnp.float32,
    )
    pair_proj = jnp.dot(
        normed,
        lax.all_gather(pair_rows, "fsdp", axis=0, tiled=True),
        preferred_element_type=jnp.float32,
    )
    positions = (offset + jnp.arange(tok_dev, dtype=jnp.int32)) % seq_length
    head_size = pair_width // 2
    query_rot = rotary(
        queries.reshape(tok_dev, query_width // head_size, head_size), positions
    ).astype(jnp.bfloat16)
    key_rot = rotary(pair_proj[:, None, :head_size], positions)[:, 0, :].astype(jnp.bfloat16)
    pair_local = jnp.concatenate([key_rot, pair_proj[:, head_size:].astype(jnp.bfloat16)], axis=1)
    pair_all = lax.all_gather(pair_local, "fsdp", axis=0, tiled=True)
    key_pos = jnp.arange(seq_length, dtype=jnp.int32)
    context = attend_heads(query_rot, pair_all, positions, key_pos)
    return context


MESH = pl.DeviceIdType.MESH
plane = 4


def fused_kernel(
    n_line, share_ref, cos_ref, sin_ref, tok_hbm, query_hbm, pair_hbm, out_ref,
    raw, nrm, mine, theirs, wbuf, tok, acc, rsend, rrecv, qrot, kvb,
    raw_sem, mine_sem, ck_s, ck_r, w_s, w_r, tl_sem, tp_s, tp_r, ts_s, ts_r,
    rs_s, rs_r, kz_s, kp_s, kb_s, kz_r, ks_r, o_s, o_r,
):
    n_fsdp = n_line * plane
    r = lax.axis_index("rep")
    f = lax.axis_index("fsdp")
    z, p = f // plane, lax.rem(f, plane)
    sib = 1 - r
    n_heads = qrot.shape[0]
    pieces = n_heads + 1
    n_tok = acc.shape[1]
    half = n_tok // 2
    head = acc.shape[2]
    depth = wbuf.shape[2]
    can_up, can_down = z < n_line - 1, z > 0
    to_sib = {"rep": sib}

    def peer(j):
        return lax.rem(p + j, plane)

    def remote(src, dst, send, recv, where):
        return pltpu.make_async_remote_copy(
            src_ref=src, dst_ref=dst, send_sem=send, recv_sem=recv,
            device_id=where, device_id_type=MESH,
        )

    def others(fn):
        for d in range(1, n_line):
            pl.when(z >= d)(functools.partial(fn, z - d, True))
            pl.when(z + d < n_line)(functools.partial(fn, z + d, False))

    raw_copy = pltpu.make_async_copy(
        tok_hbm.at[pl.ds(pl.multiple_of(r * half, half), half), :], raw, raw_sem
    )

    def columns(k, side):
        if k == 0:
            return pair_hbm.at[0, :, pl.ds(pl.multiple_of(side * head, head), head)]
        first = pl.multiple_of((side * n_heads + (k - 1)) * head, head)
        return query_hbm.at[0, :, pl.ds(first, head)]

    def own_ckpt(k):
        return pltpu.make_async_copy(columns(k, r), mine.at[k], mine_sem.at[k])

    def sib_ckpt(k):
        return remote(columns(k, sib), theirs.at[k], ck_s.at[k], ck_r.at[k], to_sib)

    own_ckpt(0).start()
    raw_copy.start()
    for k in range(1, pieces):
        own_ckpt(k).start()

    barrier = pltpu.get_barrier_semaphore()
    pl.semaphore_signal(barrier, inc=1, device_id=to_sib, device_id_type=MESH)
    for j in range(1, plane):
        pl.semaphore_signal(
            barrier, inc=1, device_id={"fsdp": z * plane + peer(j)}, device_id_type=MESH
        )

    @pl.when(can_up)
    def _():
        pl.semaphore_signal(barrier, inc=1, device_id={"fsdp": f + plane}, device_id_type=MESH)

    @pl.when(can_down)
    def _():
        pl.semaphore_signal(barrier, inc=1, device_id={"fsdp": f - plane}, device_id_type=MESH)

    pl.semaphore_wait(barrier, plane + can_up.astype(jnp.int32) + can_down.astype(jnp.int32))

    for k in range(pieces):
        sib_ckpt(k).start()

    def w_copy(k, c, up):
        return remote(
            wbuf.at[k, c], wbuf.at[k, c], w_s.at[k, c, 0 if up else 1], w_r.at[k, c],
            {"fsdp": f + plane if up else f - plane},
        )

    def average(k):
        own_ckpt(k).wait()
        sib_ckpt(k).wait_recv()
        wbuf[k, z] = (share_ref[r] * mine[k] + share_ref[sib] * theirs[k]).astype(jnp.bfloat16)

    def send_own(k):
        pl.when(can_up)(lambda: w_copy(k, z, True).start())
        pl.when(can_down)(lambda: w_copy(k, z, False).start())

    def forward(k):
        def one(c, from_below):
            w_copy(k, c, from_below).wait_recv()
            pl.when(can_up if from_below else can_down)(lambda: w_copy(k, c, from_below).start())

        others(one)

    average(0)
    send_own(0)

    raw_copy.wait()

    def norm_rows(i, carry):
        rows = pl.ds(pl.multiple_of(i * 16, 16), 16)
        wide = raw[rows, :].astype(jnp.float32)
        inv = lax.rsqrt(jnp.mean(wide * wide, axis=-1, keepdims=True) + eps_norm)
        for b in range(n_fsdp):
            part = raw[rows, b * depth : (b + 1) * depth].astype(jnp.float32)
            nrm[b, rows, :] = (part * inv).astype(jnp.bfloat16)
        return carry

    lax.fori_loop(0, half // 16, norm_rows, 0)

    def tok_rows(c, chip, side):
        first = pl.multiple_of(chip * n_tok + side * half, half)
        return tok.at[c, pl.ds(first, half), :]

    def tok_own(c):
        return pltpu.make_async_copy(nrm.at[c * plane + p], tok_rows(c, p, r), tl_sem.at[c])

    def tok_own_sib(c):
        return remote(
            nrm.at[c * plane + p], tok_rows(c, p, r), ts_s.at[c, p], ts_r.at[c, p], to_sib
        )

    def tok_peer(c, j):
        q = peer(j)
        return remote(
            nrm.at[c * plane + q], tok_rows(c, p, r), tp_s.at[c, q], tp_r.at[c, p],
            {"fsdp": z * plane + q},
        )

    def tok_arrival(c, j):
        q = peer(j)
        return remote(tok_rows(c, q, r), tok_rows(c, q, r), tp_s.at[c, q], tp_r.at[c, q], to_sib)

    def tok_pass(c, j):
        q = peer(j)
        return remote(tok_rows(c, q, r), tok_rows(c, q, r), ts_s.at[c, q], ts_r.at[c, q], to_sib)

    def tok_from_sib(c, q):
        return remote(
            tok_rows(c, q, sib), tok_rows(c, q, sib), ts_s.at[c, q], ts_r.at[c, q], to_sib
        )

    for c in range(n_line):
        for j in range(1, plane):
            tok_peer(c, j).start()
        tok_own(c).start()
        tok_own_sib(c).start()

    for k in range(1, pieces):
        average(k)
        if k <= 2:
            send_own(k)

    forward(0)
    send_own(3)
    forward(1)
    send_own(4)

    for c in range(n_line):
        for j in range(1, plane):
            tok_arrival(c, j).wait_recv()
            tok_pass(c, j).start()
    for c in range(n_line):
        tok_own(c).wait()
        for q in range(plane):
            tok_from_sib(c, q).wait_recv()

    def rs_copy(k, j):
        q = peer(j)
        return remote(
            rsend.at[k, q], rrecv.at[k, p], rs_s.at[k, q], rs_r.at[k, p],
            {"fsdp": z * plane + q},
        )

    def rs_arrival(k, j):
        q = peer(j)
        return remote(rrecv.at[k, q], rrecv.at[k, q], rs_s.at[k, q], rs_r.at[k, q], to_sib)

    def multiply(k):
        for j in (2, 1, 3, 0):
            q = peer(j)
            rows = pl.ds(pl.multiple_of(q * n_tok, n_tok), n_tok)
            part = jnp.dot(tok[0, rows, :], wbuf[k, 0], preferred_element_type=jnp.float32)
            for c in range(1, n_line):
                part += jnp.dot(tok[c, rows, :], wbuf[k, c], preferred_element_type=jnp.float32)
            if j:
                rsend[k, q] = part.astype(jnp.bfloat16)
                rs_copy(k, j).start()
            else:
                acc[k] = part

    def total(k):
        value = acc[k]
        for j in range(1, plane):
            rs_arrival(k, j).wait_recv()
            value += rrecv[k, peer(j)].astype(jnp.float32)
        return value

    def rotate(value):
        return value * cos_ref[...] + pltpu.roll(value, head // 2, 1) * sin_ref[...]

    def kv_rows(b, side):
        return kvb.at[side, pl.ds(pl.multiple_of(b * n_tok, n_tok), n_tok), :]

    def kv_line(c, up):
        b = c * plane + p
        return remote(
            kv_rows(b, r), kv_rows(b, r), kz_s.at[c, 0 if up else 1], kz_r.at[b],
            {"fsdp": f + plane if up else f - plane},
        )

    def kv_plane(c, j):
        b = c * plane + p
        return remote(
            kv_rows(b, r), kv_rows(b, r), kp_s.at[c, peer(j)], kz_r.at[b],
            {"fsdp": z * plane + peer(j)},
        )

    def kv_sib(b):
        return remote(kv_rows(b, r), kv_rows(b, r), kb_s.at[b], ks_r.at[b], to_sib)

    def kv_from_sib(b):
        return remote(kv_rows(b, sib), kv_rows(b, sib), kb_s.at[b], ks_r.at[b], to_sib)

    def kv_arrival(b):
        return remote(kv_rows(b, r), kv_rows(b, r), kb_s.at[b], kz_r.at[b], to_sib)

    def kv_spread(c):
        for j in range(1, plane):
            kv_plane(c, j).start()
        kv_sib(c * plane + p).start()

    def kv_begin():
        value = total(0)
        value = jnp.where(r == 0, rotate(value), value)
        kvb[r, pl.ds(pl.multiple_of(f * n_tok, n_tok), n_tok), :] = value.astype(jnp.bfloat16)
        pl.when(can_up)(lambda: kv_line(z, True).start())
        pl.when(can_down)(lambda: kv_line(z, False).start())
        kv_spread(z)

    def kv_middle():
        def one(c, from_below):
            kv_arrival(c * plane + p).wait_recv()
            pl.when(can_up if from_below else can_down)(lambda: kv_line(c, from_below).start())
            kv_spread(c)

        others(one)

    def kv_end():
        for c in range(n_line):
            for j in range(1, plane):
                b = c * plane + peer(j)
                kv_arrival(b).wait_recv()
                kv_sib(b).start()
        for b in range(n_fsdp):
            kv_from_sib(b).wait_recv()

    block = 2 * n_tok
    scale = math.log2(math.e) / math.sqrt(head)

    def out_copy(h, side):
        col = pl.ds(pl.multiple_of((side * n_heads + h) * head, head), head)
        return remote(out_ref.at[:, col], out_ref.at[:, col], o_s.at[h], o_r.at[h], to_sib)

    def query(h):
        qrot[h] = rotate(total(h + 1)).astype(jnp.bfloat16)

    def attend(h):
        q = qrot[h]

        def step(i, carry, masked):
            top, norm, mixed = carry
            rows = pl.ds(pl.multiple_of(i * block, block), block)
            scores = lax.dot_general(
                q, kvb[0, rows, :], (((1,), (1,)), ((), ())), preferred_element_type=jnp.float32
            )
            if masked:
                row = lax.broadcasted_iota(jnp.int32, scores.shape, 0) + f * n_tok
                col = lax.broadcasted_iota(jnp.int32, scores.shape, 1) + i * block
                scores = jnp.where(col <= row, scores, masked_score)
            new_top = jnp.maximum(top, jnp.max(scores, axis=1, keepdims=True))
            weights = jnp.exp2((scores - new_top) * scale)
            fade = jnp.exp2((top - new_top) * scale)
            norm = norm * fade + jnp.sum(weights, axis=1, keepdims=True)
            mixed = mixed * fade + jnp.dot(
                weights.astype(jnp.bfloat16), kvb[1, rows, :], preferred_element_type=jnp.float32
            )
            return new_top, norm, mixed

        last = (f * n_tok) // block
        carry = (
            jnp.full((n_tok, 1), masked_score, jnp.float32),
            jnp.zeros((n_tok, 1), jnp.float32),
            jnp.zeros((n_tok, head), jnp.float32),
        )
        carry = step(last, carry, True)
        _, norm, mixed = lax.fori_loop(0, last, functools.partial(step, masked=False), carry)
        col = pl.ds(pl.multiple_of((r * n_heads + h) * head, head), head)
        out_ref[:, col] = (mixed / norm).astype(jnp.bfloat16)
        out_copy(h, r).start()

    multiply(0)
    multiply(1)
    kv_begin()
    forward(2)
    multiply(2)
    kv_middle()
    forward(3)
    multiply(3)
    query(0)
    query(1)
    kv_end()
    attend(0)
    forward(4)
    multiply(4)
    attend(1)
    query(2)
    attend(2)
    query(3)
    attend(3)

    for k in range(pieces):
        sib_ckpt(k).wait_send()
        pl.when(can_up)(lambda k=k: w_copy(k, z, True).wait_send())
        pl.when(can_down)(lambda k=k: w_copy(k, z, False).wait_send())

        def sent(c, from_below, k=k):
            ok = can_up if from_below else can_down
            pl.when(ok)(lambda: w_copy(k, c, from_below).wait_send())

        others(sent)
        for j in range(1, plane):
            rs_copy(k, j).wait_send()
    for c in range(n_line):
        tok_own_sib(c).wait_send()
        for j in range(1, plane):
            tok_peer(c, j).wait_send()
            tok_pass(c, j).wait_send()
            kv_plane(c, j).wait_send()
    pl.when(can_up)(lambda: kv_line(z, True).wait_send())
    pl.when(can_down)(lambda: kv_line(z, False).wait_send())

    def kv_sent(c, from_below):
        ok = can_up if from_below else can_down
        pl.when(ok)(lambda: kv_line(c, from_below).wait_send())

    others(kv_sent)
    for b in range(n_fsdp):
        kv_sib(b).wait_send()
    for h in range(n_heads):
        out_copy(h, r).wait_send()
        out_copy(h, sib).wait_recv()


def fused_local(tokens, query_ckpt, key_value_ckpt, numerators):
    n_fsdp = lax.axis_size("fsdp")
    n_line = n_fsdp // plane
    n_tok, width = tokens.shape
    depth, query_width = query_ckpt.shape[1:]
    head = key_value_ckpt.shape[2] // 2
    n_heads = query_width // head // 2
    pieces = n_heads + 1
    half = n_tok // 2
    shares = numerators.astype(jnp.float32) / jnp.sum(numerators).astype(jnp.float32)
    positions = lax.axis_index("fsdp") * n_tok + jnp.arange(n_tok, dtype=jnp.int32)
    inverse_freq = jnp.exp(
        -(jnp.arange(head // 2, dtype=jnp.float32) * (2.0 / head)) * math.log(theta_base)
    )
    angles = positions.astype(jnp.float32)[:, None] * inverse_freq[None, :]
    cosine, sine = jnp.cos(angles), jnp.sin(angles)
    cos_table = jnp.concatenate([cosine, cosine], axis=1)
    sin_table = jnp.concatenate([-sine, sine], axis=1)
    vmem, bf16, f32 = pltpu.VMEM, jnp.bfloat16, jnp.float32
    dma = pltpu.SemaphoreType.DMA
    return pl.pallas_call(
        functools.partial(fused_kernel, n_line),
        out_shape=jax.ShapeDtypeStruct((n_tok, query_width), bf16),
        in_specs=[
            pl.BlockSpec(memory_space=pltpu.SMEM),
            pl.BlockSpec(memory_space=pltpu.VMEM),
            pl.BlockSpec(memory_space=pltpu.VMEM),
            pl.BlockSpec(memory_space=pl.ANY),
            pl.BlockSpec(memory_space=pl.ANY),
            pl.BlockSpec(memory_space=pl.ANY),
        ],
        out_specs=pl.BlockSpec(memory_space=pltpu.VMEM),
        scratch_shapes=[
            vmem((half, width), bf16),
            vmem((n_fsdp, half, depth), bf16),
            vmem((pieces, depth, head), f32),
            vmem((pieces, depth, head), f32),
            vmem((pieces, n_line, depth, head), bf16),
            vmem((n_line, plane * n_tok, depth), bf16),
            vmem((pieces, n_tok, head), f32),
            vmem((pieces, plane, n_tok, head), bf16),
            vmem((pieces, plane, n_tok, head), bf16),
            vmem((n_heads, n_tok, head), bf16),
            vmem((2, n_fsdp * n_tok, head), bf16),
            dma,
            dma((pieces,)),
            dma((pieces,)),
            dma((pieces,)),
            dma((pieces, n_line, 2)),
            dma((pieces, n_line)),
            dma((n_line,)),
            dma((n_line, plane)),
            dma((n_line, plane)),
            dma((n_line, plane)),
            dma((n_line, plane)),
            dma((pieces, plane)),
            dma((pieces, plane)),
            dma((n_line, 2)),
            dma((n_line, plane)),
            dma((n_fsdp,)),
            dma((n_fsdp,)),
            dma((n_fsdp,)),
            dma((n_heads,)),
            dma((n_heads,)),
        ],
        compiler_params=pltpu.CompilerParams(
            collective_id=0, has_side_effects=True, vmem_limit_bytes=48 * 1024 * 1024
        ),
        cost_estimate=pl.CostEstimate(
            flops=2 * n_tok * width * query_width, bytes_accessed=8 * depth * query_width,
            transcendentals=n_heads * n_tok * n_tok * n_fsdp,
        ),
    )(shares, cos_table, sin_table, tokens, query_ckpt, key_value_ckpt)


def solution(mesh):
    in_specs = (P("fsdp", None), P("rep", "fsdp", None), P("rep", "fsdp", None), P())
    out_specs = P("fsdp", None)
    paired = mesh.shape["rep"] == 2 and mesh.shape["fsdp"] % plane == 0
    body = fused_local if paired else local
    return jax.shard_map(body, mesh=mesh, in_specs=in_specs, out_specs=out_specs, check_vma=False)
```

```python
import math

import functools

import jax
import jax.numpy as jnp
from jax import lax
from jax.experimental import pallas as pl
from jax.experimental.pallas import tpu as pltpu
from jax.sharding import PartitionSpec as P

theta_base = 500000.0
eps_norm = 1e-05
masked_score = -1e30


def rms_normed(hidden):
    wide_copy = hidden.astype(jnp.float32)
    return (
        wide_copy * lax.rsqrt(jnp.mean(wide_copy * wide_copy, axis=-1, keepdims=True) + eps_norm)
    ).astype(jnp.bfloat16)


def rotary(values, positions):
    half_size = values.shape[-1] // 2
    inverse_freq = jnp.exp(
        -(jnp.arange(half_size, dtype=jnp.float32) * (2.0 / values.shape[-1]))
        * math.log(theta_base)
    )
    angles = positions.astype(jnp.float32)[:, None] * inverse_freq[None, :]
    cosine_table = jnp.cos(angles)[:, None, :]
    sine_table = jnp.sin(angles)[:, None, :]
    first_half = values[..., :half_size]
    second_half = values[..., half_size:]
    return jnp.concatenate(
        [
            first_half * cosine_table - second_half * sine_table,
            second_half * cosine_table + first_half * sine_table,
        ],
        axis=-1,
    )


def attend_heads(queries, pair_rows, query_pos, key_pos):
    head_size = queries.shape[-1]
    key_rows = pair_rows[:, :head_size]
    value_rows = pair_rows[:, head_size:]
    score_scale = 1.0 / math.sqrt(head_size)
    allowed = key_pos[None, :] <= query_pos[:, None]

    def one_head(query_head):
        scores = jnp.dot(query_head, key_rows.T, preferred_element_type=jnp.float32) * score_scale
        scores = jnp.where(allowed, scores, masked_score)
        row_top = jnp.max(scores, axis=1, keepdims=True)
        weights_exp = jnp.exp(scores - row_top)
        norm_sum = jnp.sum(weights_exp, axis=1, keepdims=True)
        mixed_out = (
            jnp.dot(
                weights_exp.astype(jnp.bfloat16), value_rows, preferred_element_type=jnp.float32
            )
            / norm_sum
        )
        return mixed_out.astype(jnp.bfloat16)

    head_outs = lax.map(one_head, jnp.transpose(queries, (1, 0, 2)))
    return jnp.transpose(head_outs, (1, 0, 2)).reshape(queries.shape[0], -1)


def local(tokens, query_ckpt, key_value_ckpt, numerators):
    fsdp_count = lax.axis_size("fsdp")
    rep_idx = lax.axis_index("rep")
    fsdp_idx = lax.axis_index("fsdp")
    slot_ids = jnp.arange(numerators.shape[0], dtype=jnp.int32)
    weight_sum = jnp.sum(numerators).astype(jnp.float32)
    my_share = (
        jnp.sum(jnp.where(slot_ids == rep_idx, numerators, 0)).astype(jnp.float32) / weight_sum
    )
    query_term = my_share * query_ckpt[0]
    pair_term = my_share * key_value_ckpt[0]
    tok_dev = tokens.shape[0]
    seq_length = tok_dev * fsdp_count
    offset = fsdp_idx * tok_dev
    normed = rms_normed(tokens)
    query_width = query_ckpt.shape[2]
    pair_width = key_value_ckpt.shape[2]
    query_sum, pair_sum = lax.psum((query_term, pair_term), "rep")
    query_rows = query_sum.astype(jnp.bfloat16)
    pair_rows = pair_sum.astype(jnp.bfloat16)
    queries = jnp.dot(
        normed,
        lax.all_gather(query_rows, "fsdp", axis=0, tiled=True),
        preferred_element_type=jnp.float32,
    )
    pair_proj = jnp.dot(
        normed,
        lax.all_gather(pair_rows, "fsdp", axis=0, tiled=True),
        preferred_element_type=jnp.float32,
    )
    positions = (offset + jnp.arange(tok_dev, dtype=jnp.int32)) % seq_length
    head_size = pair_width // 2
    query_rot = rotary(
        queries.reshape(tok_dev, query_width // head_size, head_size), positions
    ).astype(jnp.bfloat16)
    key_rot = rotary(pair_proj[:, None, :head_size], positions)[:, 0, :].astype(jnp.bfloat16)
    pair_local = jnp.concatenate([key_rot, pair_proj[:, head_size:].astype(jnp.bfloat16)], axis=1)
    pair_all = lax.all_gather(pair_local, "fsdp", axis=0, tiled=True)
    key_pos = jnp.arange(seq_length, dtype=jnp.int32)
    context = attend_heads(query_rot, pair_all, positions, key_pos)
    return context


MESH = pl.DeviceIdType.MESH
plane = 4


def fused_kernel(
    n_line, num_ref, cos_ref, sin_ref, tok_hbm, query_hbm, pair_hbm, out_ref,
    raw, inv_rms, nrm, mine, theirs, wbuf, tok, acc, rsend, rrecv, qrot, kvb,
    raw_sem, mine_sem, ck_s, ck_r, w_s, w_r, tl_sem, tp_s, tp_r, ts_s, ts_r,
    rs_s, rs_r, kz_s, kp_s, kb_s, kz_r, ks_r, o_s, o_r,
):
    n_fsdp = n_line * plane
    r = lax.axis_index("rep")
    f = lax.axis_index("fsdp")
    z, p = f // plane, lax.rem(f, plane)
    sib = 1 - r
    n_heads = qrot.shape[0]
    pieces = n_heads + 1
    n_tok = acc.shape[1]
    half = n_tok // 2
    head = acc.shape[2]
    depth = wbuf.shape[2]
    can_up, can_down = z < n_line - 1, z > 0
    to_sib = {"rep": sib}

    def peer(j):
        return lax.rem(p + j, plane)

    def remote(src, dst, send, recv, where):
        return pltpu.make_async_remote_copy(
            src_ref=src, dst_ref=dst, send_sem=send, recv_sem=recv,
            device_id=where, device_id_type=MESH,
        )

    def others(fn, lo=1, hi=n_line):
        for d in range(lo, hi):
            pl.when(z >= d)(functools.partial(fn, z - d, True))
            pl.when(z + d < n_line)(functools.partial(fn, z + d, False))

    raw_copy = pltpu.make_async_copy(
        tok_hbm.at[pl.ds(pl.multiple_of(r * half, half), half), :], raw, raw_sem
    )

    def columns(k, side):
        if k == 0:
            return pair_hbm.at[0, :, pl.ds(pl.multiple_of(side * head, head), head)]
        first = pl.multiple_of((side * n_heads + (k - 1)) * head, head)
        return query_hbm.at[0, :, pl.ds(first, head)]

    def own_ckpt(k):
        return pltpu.make_async_copy(columns(k, r), mine.at[k], mine_sem.at[k])

    def sib_ckpt(k):
        return remote(columns(k, sib), theirs.at[k], ck_s.at[k], ck_r.at[k], to_sib)

    own_ckpt(0).start()
    raw_copy.start()
    for k in range(1, pieces):
        own_ckpt(k).start()

    barrier = pltpu.get_barrier_semaphore()
    pl.semaphore_signal(barrier, inc=1, device_id=to_sib, device_id_type=MESH)
    for j in range(1, plane):
        pl.semaphore_signal(
            barrier, inc=1, device_id={"fsdp": z * plane + peer(j)}, device_id_type=MESH
        )

    @pl.when(can_up)
    def _():
        pl.semaphore_signal(barrier, inc=1, device_id={"fsdp": f + plane}, device_id_type=MESH)

    @pl.when(can_down)
    def _():
        pl.semaphore_signal(barrier, inc=1, device_id={"fsdp": f - plane}, device_id_type=MESH)

    pl.semaphore_wait(barrier, plane + can_up.astype(jnp.int32) + can_down.astype(jnp.int32))

    for k in range(pieces):
        sib_ckpt(k).start()

    def w_copy(k, c, up):
        return remote(
            wbuf.at[k, c], wbuf.at[k, c], w_s.at[k, c, 0 if up else 1], w_r.at[k, c],
            {"fsdp": f + plane if up else f - plane},
        )

    def share(side):
        whole = (num_ref[0] + num_ref[1]).astype(jnp.float32)
        return jnp.full((1, head), num_ref[side].astype(jnp.float32)) / jnp.full((1, head), whole)

    def average(k):
        own_ckpt(k).wait()
        sib_ckpt(k).wait_recv()
        wbuf[k, z] = (share(r) * mine[k] + share(sib) * theirs[k]).astype(jnp.bfloat16)

    def send_own(k):
        pl.when(can_up)(lambda: w_copy(k, z, True).start())
        pl.when(can_down)(lambda: w_copy(k, z, False).start())

    def forward(k, lo=1, hi=n_line):
        def one(c, from_below):
            w_copy(k, c, from_below).wait_recv()
            pl.when(can_up if from_below else can_down)(lambda: w_copy(k, c, from_below).start())

        others(one, lo, hi)

    def near(k):
        forward(k, 1, min(2, n_line))

    def middle(k):
        forward(k, 2, n_line - 1)

    def far(k):
        forward(k, max(2, n_line - 1), n_line)

    def tok_rows(c, chip, side):
        first = pl.multiple_of(chip * n_tok + side * half, half)
        return tok.at[c, pl.ds(first, half), :]

    def tok_own(c):
        return pltpu.make_async_copy(nrm.at[c * plane + p], tok_rows(c, p, r), tl_sem.at[c])

    def tok_own_sib(c):
        return remote(
            nrm.at[c * plane + p], tok_rows(c, p, r), ts_s.at[c, p], ts_r.at[c, p], to_sib
        )

    def tok_peer(c, j):
        q = peer(j)
        return remote(
            nrm.at[c * plane + q], tok_rows(c, p, r), tp_s.at[c, q], tp_r.at[c, p],
            {"fsdp": z * plane + q},
        )

    def tok_arrival(c, j):
        q = peer(j)
        return remote(tok_rows(c, q, r), tok_rows(c, q, r), tp_s.at[c, q], tp_r.at[c, q], to_sib)

    def tok_pass(c, j):
        q = peer(j)
        return remote(tok_rows(c, q, r), tok_rows(c, q, r), ts_s.at[c, q], ts_r.at[c, q], to_sib)

    def tok_from_sib(c, q):
        return remote(
            tok_rows(c, q, sib), tok_rows(c, q, sib), ts_s.at[c, q], ts_r.at[c, q], to_sib
        )

    def inverse_rms(i, carry):
        rows = pl.ds(pl.multiple_of(i * 16, 16), 16)
        wide = raw[rows, :].astype(jnp.float32)
        inv = lax.rsqrt(jnp.mean(wide * wide, axis=-1, keepdims=True) + eps_norm)
        inv_rms[rows, :] = jnp.broadcast_to(inv, (16, inv_rms.shape[1]))
        return carry

    def norm_send(c):
        def norm_rows(i, carry):
            rows = pl.ds(pl.multiple_of(i * 16, 16), 16)
            inv = inv_rms[rows, :1]
            for b in range(c * plane, (c + 1) * plane):
                part = raw[rows, b * depth : (b + 1) * depth].astype(jnp.float32)
                nrm[b, rows, :] = (part * inv).astype(jnp.bfloat16)
            return carry

        lax.fori_loop(0, half // 16, norm_rows, 0)
        for j in (2, 1, 3):
            tok_peer(c, j).start()
        tok_own(c).start()
        tok_own_sib(c).start()

    def tok_collect(c):
        for j in range(1, plane):
            tok_arrival(c, j).wait_recv()
            tok_pass(c, j).start()

    average(0)
    send_own(0)
    raw_copy.wait()
    lax.fori_loop(0, half // 16, inverse_rms, 0)
    average(1)
    send_own(1)
    norm_send(0)
    near(0)
    for k in range(2, pieces):
        average(k)
        send_own(k)
        if k - 1 < n_line:
            norm_send(k - 1)
    for c in range(pieces - 1, n_line):
        norm_send(c)
    middle(0)
    for k in range(1, pieces):
        near(k)
    for c in range(n_line):
        tok_collect(c)
        if c + 1 < pieces:
            middle(c + 1)
    for k in range(n_line + 1, pieces):
        middle(k)
    for c in range(n_line):
        tok_own(c).wait()
        for q in range(plane):
            tok_from_sib(c, q).wait_recv()

    def rs_copy(k, j):
        q = peer(j)
        return remote(
            rsend.at[k, q], rrecv.at[k, p], rs_s.at[k, q], rs_r.at[k, p],
            {"fsdp": z * plane + q},
        )

    def rs_arrival(k, j):
        q = peer(j)
        return remote(rrecv.at[k, q], rrecv.at[k, q], rs_s.at[k, q], rs_r.at[k, q], to_sib)

    def multiply(k):
        for j in (2, 1, 3, 0):
            q = peer(j)
            rows = pl.ds(pl.multiple_of(q * n_tok, n_tok), n_tok)
            part = jnp.dot(tok[0, rows, :], wbuf[k, 0], preferred_element_type=jnp.float32)
            for c in range(1, n_line):
                part += jnp.dot(tok[c, rows, :], wbuf[k, c], preferred_element_type=jnp.float32)
            if j:
                rsend[k, q] = part.astype(jnp.bfloat16)
                rs_copy(k, j).start()
            else:
                acc[k] = part

    def total(k):
        value = acc[k]
        for j in range(1, plane):
            rs_arrival(k, j).wait_recv()
            value += rrecv[k, peer(j)].astype(jnp.float32)
        return value

    def rotate(value):
        return value * cos_ref[...] + pltpu.roll(value, head // 2, 1) * sin_ref[...]

    def kv_rows(b, side):
        return kvb.at[side, pl.ds(pl.multiple_of(b * n_tok, n_tok), n_tok), :]

    def kv_line(c, up):
        b = c * plane + p
        return remote(
            kv_rows(b, r), kv_rows(b, r), kz_s.at[c, 0 if up else 1], kz_r.at[b],
            {"fsdp": f + plane if up else f - plane},
        )

    def kv_plane(c, j):
        b = c * plane + p
        return remote(
            kv_rows(b, r), kv_rows(b, r), kp_s.at[c, peer(j)], kz_r.at[b],
            {"fsdp": z * plane + peer(j)},
        )

    def kv_sib(b):
        return remote(kv_rows(b, r), kv_rows(b, r), kb_s.at[b], ks_r.at[b], to_sib)

    def kv_from_sib(b):
        return remote(kv_rows(b, sib), kv_rows(b, sib), kb_s.at[b], ks_r.at[b], to_sib)

    def kv_arrival(b):
        return remote(kv_rows(b, r), kv_rows(b, r), kb_s.at[b], kz_r.at[b], to_sib)

    def kv_spread(c):
        for j in range(1, plane):
            kv_plane(c, j).start()
        kv_sib(c * plane + p).start()

    def kv_begin():
        value = total(0)
        value = jnp.where(r == 0, rotate(value), value)
        kvb[r, pl.ds(pl.multiple_of(f * n_tok, n_tok), n_tok), :] = value.astype(jnp.bfloat16)
        pl.when(can_up)(lambda: kv_line(z, True).start())
        pl.when(can_down)(lambda: kv_line(z, False).start())
        kv_spread(z)

    def kv_step(lo, hi):
        def one(c, from_below):
            kv_arrival(c * plane + p).wait_recv()
            pl.when(can_up if from_below else can_down)(lambda: kv_line(c, from_below).start())
            kv_spread(c)

        others(one, lo, hi)

    def kv_end():
        for c in range(n_line):
            for j in range(1, plane):
                b = c * plane + peer(j)
                kv_arrival(b).wait_recv()
                kv_sib(b).start()
        for b in range(n_fsdp):
            kv_from_sib(b).wait_recv()

    block = 2 * n_tok
    scale = math.log2(math.e) / math.sqrt(head)

    def out_copy(h, side):
        col = pl.ds(pl.multiple_of((side * n_heads + h) * head, head), head)
        return remote(out_ref.at[:, col], out_ref.at[:, col], o_s.at[h], o_r.at[h], to_sib)

    def query(h):
        qrot[h] = rotate(total(h + 1)).astype(jnp.bfloat16)

    def attend(h):
        q = qrot[h]

        def step(i, carry, masked):
            top, norm, mixed = carry
            rows = pl.ds(pl.multiple_of(i * block, block), block)
            scores = lax.dot_general(
                q, kvb[0, rows, :], (((1,), (1,)), ((), ())), preferred_element_type=jnp.float32
            )
            if masked:
                row = lax.broadcasted_iota(jnp.int32, scores.shape, 0) + f * n_tok
                col = lax.broadcasted_iota(jnp.int32, scores.shape, 1) + i * block
                scores = jnp.where(col <= row, scores, masked_score)
            new_top = jnp.maximum(top, jnp.max(scores, axis=1, keepdims=True))
            weights = jnp.exp2((scores - new_top) * scale)
            fade = jnp.exp2((top - new_top) * scale)
            norm = norm * fade + jnp.sum(weights, axis=1, keepdims=True)
            mixed = mixed * fade + jnp.dot(
                weights.astype(jnp.bfloat16), kvb[1, rows, :], preferred_element_type=jnp.float32
            )
            return new_top, norm, mixed

        last = (f * n_tok) // block
        carry = (
            jnp.full((n_tok, 1), masked_score, jnp.float32),
            jnp.zeros((n_tok, 1), jnp.float32),
            jnp.zeros((n_tok, head), jnp.float32),
        )
        carry = step(last, carry, True)
        _, norm, mixed = lax.fori_loop(0, last, functools.partial(step, masked=False), carry)
        col = pl.ds(pl.multiple_of((r * n_heads + h) * head, head), head)
        out_ref[:, col] = (mixed / norm).astype(jnp.bfloat16)
        out_copy(h, r).start()

    far(0)
    multiply(0)
    far(1)
    multiply(1)
    kv_begin()
    far(2)
    multiply(2)
    kv_step(1, min(2, n_line))
    far(3)
    multiply(3)
    kv_step(2, n_line)
    far(4)
    multiply(4)
    query(0)
    query(1)
    query(2)
    kv_end()
    attend(0)
    attend(1)
    attend(2)
    query(3)
    attend(3)

    for k in range(pieces):
        sib_ckpt(k).wait_send()
        pl.when(can_up)(lambda k=k: w_copy(k, z, True).wait_send())
        pl.when(can_down)(lambda k=k: w_copy(k, z, False).wait_send())

        def sent(c, from_below, k=k):
            ok = can_up if from_below else can_down
            pl.when(ok)(lambda: w_copy(k, c, from_below).wait_send())

        others(sent)
        for j in range(1, plane):
            rs_copy(k, j).wait_send()
    for c in range(n_line):
        tok_own_sib(c).wait_send()
        for j in range(1, plane):
            tok_peer(c, j).wait_send()
            tok_pass(c, j).wait_send()
            kv_plane(c, j).wait_send()
    pl.when(can_up)(lambda: kv_line(z, True).wait_send())
    pl.when(can_down)(lambda: kv_line(z, False).wait_send())

    def kv_sent(c, from_below):
        ok = can_up if from_below else can_down
        pl.when(ok)(lambda: kv_line(c, from_below).wait_send())

    others(kv_sent)
    for b in range(n_fsdp):
        kv_sib(b).wait_send()
    for h in range(n_heads):
        out_copy(h, r).wait_send()
        out_copy(h, sib).wait_recv()


def fused_local(tokens, query_ckpt, key_value_ckpt, numerators):
    n_fsdp = lax.axis_size("fsdp")
    n_line = n_fsdp // plane
    n_tok, width = tokens.shape
    depth, query_width = query_ckpt.shape[1:]
    head = key_value_ckpt.shape[2] // 2
    n_heads = query_width // head // 2
    pieces = n_heads + 1
    half = n_tok // 2
    positions = lax.axis_index("fsdp") * n_tok + jnp.arange(n_tok, dtype=jnp.int32)
    inverse_freq = jnp.exp(
        -(jnp.arange(head // 2, dtype=jnp.float32) * (2.0 / head)) * math.log(theta_base)
    )
    angles = positions.astype(jnp.float32)[:, None] * inverse_freq[None, :]
    cosine, sine = jnp.cos(angles), jnp.sin(angles)
    cos_table = jnp.concatenate([cosine, cosine], axis=1)
    sin_table = jnp.concatenate([-sine, sine], axis=1)
    vmem, bf16, f32 = pltpu.VMEM, jnp.bfloat16, jnp.float32
    dma = pltpu.SemaphoreType.DMA
    return pl.pallas_call(
        functools.partial(fused_kernel, n_line),
        out_shape=jax.ShapeDtypeStruct((n_tok, query_width), bf16),
        in_specs=[
            pl.BlockSpec(memory_space=pltpu.SMEM),
            pl.BlockSpec(memory_space=pltpu.VMEM),
            pl.BlockSpec(memory_space=pltpu.VMEM),
            pl.BlockSpec(memory_space=pl.ANY),
            pl.BlockSpec(memory_space=pl.ANY),
            pl.BlockSpec(memory_space=pl.ANY),
        ],
        out_specs=pl.BlockSpec(memory_space=pltpu.VMEM),
        scratch_shapes=[
            vmem((half, width), bf16),
            vmem((half, head), f32),
            vmem((n_fsdp, half, depth), bf16),
            vmem((pieces, depth, head), f32),
            vmem((pieces, depth, head), f32),
            vmem((pieces, n_line, depth, head), bf16),
            vmem((n_line, plane * n_tok, depth), bf16),
            vmem((pieces, n_tok, head), f32),
            vmem((pieces, plane, n_tok, head), bf16),
            vmem((pieces, plane, n_tok, head), bf16),
            vmem((n_heads, n_tok, head), bf16),
            vmem((2, n_fsdp * n_tok, head), bf16),
            dma,
            dma((pieces,)),
            dma((pieces,)),
            dma((pieces,)),
            dma((pieces, n_line, 2)),
            dma((pieces, n_line)),
            dma((n_line,)),
            dma((n_line, plane)),
            dma((n_line, plane)),
            dma((n_line, plane)),
            dma((n_line, plane)),
            dma((pieces, plane)),
            dma((pieces, plane)),
            dma((n_line, 2)),
            dma((n_line, plane)),
            dma((n_fsdp,)),
            dma((n_fsdp,)),
            dma((n_fsdp,)),
            dma((n_heads,)),
            dma((n_heads,)),
        ],
        compiler_params=pltpu.CompilerParams(
            collective_id=0, has_side_effects=True, vmem_limit_bytes=58 * 1024 * 1024
        ),
        cost_estimate=pl.CostEstimate(
            flops=2 * n_tok * width * query_width, bytes_accessed=8 * depth * query_width,
            transcendentals=n_heads * n_tok * n_tok * n_fsdp,
        ),
    )(numerators, cos_table, sin_table, tokens, query_ckpt, key_value_ckpt)


def solution(mesh):
    in_specs = (P("fsdp", None), P("rep", "fsdp", None), P("rep", "fsdp", None), P())
    out_specs = P("fsdp", None)
    paired = mesh.shape["rep"] == 2 and mesh.shape["fsdp"] % plane == 0
    body = fused_local if paired else local
    return jax.shard_map(body, mesh=mesh, in_specs=in_specs, out_specs=out_specs, check_vma=False)
```

```python
import math

import functools

import jax
import jax.numpy as jnp
from jax import lax
from jax.experimental import pallas as pl
from jax.experimental.pallas import tpu as pltpu
from jax.sharding import PartitionSpec as P

theta_base = 500000.0
eps_norm = 1e-05
masked_score = -1e30


def rms_normed(hidden):
    wide_copy = hidden.astype(jnp.float32)
    return (
        wide_copy * lax.rsqrt(jnp.mean(wide_copy * wide_copy, axis=-1, keepdims=True) + eps_norm)
    ).astype(jnp.bfloat16)


def rotary(values, positions):
    half_size = values.shape[-1] // 2
    inverse_freq = jnp.exp(
        -(jnp.arange(half_size, dtype=jnp.float32) * (2.0 / values.shape[-1]))
        * math.log(theta_base)
    )
    angles = positions.astype(jnp.float32)[:, None] * inverse_freq[None, :]
    cosine_table = jnp.cos(angles)[:, None, :]
    sine_table = jnp.sin(angles)[:, None, :]
    first_half = values[..., :half_size]
    second_half = values[..., half_size:]
    return jnp.concatenate(
        [
            first_half * cosine_table - second_half * sine_table,
            second_half * cosine_table + first_half * sine_table,
        ],
        axis=-1,
    )


def attend_heads(queries, pair_rows, query_pos, key_pos):
    head_size = queries.shape[-1]
    key_rows = pair_rows[:, :head_size]
    value_rows = pair_rows[:, head_size:]
    score_scale = 1.0 / math.sqrt(head_size)
    allowed = key_pos[None, :] <= query_pos[:, None]

    def one_head(query_head):
        scores = jnp.dot(query_head, key_rows.T, preferred_element_type=jnp.float32) * score_scale
        scores = jnp.where(allowed, scores, masked_score)
        row_top = jnp.max(scores, axis=1, keepdims=True)
        weights_exp = jnp.exp(scores - row_top)
        norm_sum = jnp.sum(weights_exp, axis=1, keepdims=True)
        mixed_out = (
            jnp.dot(
                weights_exp.astype(jnp.bfloat16), value_rows, preferred_element_type=jnp.float32
            )
            / norm_sum
        )
        return mixed_out.astype(jnp.bfloat16)

    head_outs = lax.map(one_head, jnp.transpose(queries, (1, 0, 2)))
    return jnp.transpose(head_outs, (1, 0, 2)).reshape(queries.shape[0], -1)


def local(tokens, query_ckpt, key_value_ckpt, numerators):
    fsdp_count = lax.axis_size("fsdp")
    rep_idx = lax.axis_index("rep")
    fsdp_idx = lax.axis_index("fsdp")
    slot_ids = jnp.arange(numerators.shape[0], dtype=jnp.int32)
    weight_sum = jnp.sum(numerators).astype(jnp.float32)
    my_share = (
        jnp.sum(jnp.where(slot_ids == rep_idx, numerators, 0)).astype(jnp.float32) / weight_sum
    )
    query_term = my_share * query_ckpt[0]
    pair_term = my_share * key_value_ckpt[0]
    tok_dev = tokens.shape[0]
    seq_length = tok_dev * fsdp_count
    offset = fsdp_idx * tok_dev
    normed = rms_normed(tokens)
    query_width = query_ckpt.shape[2]
    pair_width = key_value_ckpt.shape[2]
    query_sum, pair_sum = lax.psum((query_term, pair_term), "rep")
    query_rows = query_sum.astype(jnp.bfloat16)
    pair_rows = pair_sum.astype(jnp.bfloat16)
    queries = jnp.dot(
        normed,
        lax.all_gather(query_rows, "fsdp", axis=0, tiled=True),
        preferred_element_type=jnp.float32,
    )
    pair_proj = jnp.dot(
        normed,
        lax.all_gather(pair_rows, "fsdp", axis=0, tiled=True),
        preferred_element_type=jnp.float32,
    )
    positions = (offset + jnp.arange(tok_dev, dtype=jnp.int32)) % seq_length
    head_size = pair_width // 2
    query_rot = rotary(
        queries.reshape(tok_dev, query_width // head_size, head_size), positions
    ).astype(jnp.bfloat16)
    key_rot = rotary(pair_proj[:, None, :head_size], positions)[:, 0, :].astype(jnp.bfloat16)
    pair_local = jnp.concatenate([key_rot, pair_proj[:, head_size:].astype(jnp.bfloat16)], axis=1)
    pair_all = lax.all_gather(pair_local, "fsdp", axis=0, tiled=True)
    key_pos = jnp.arange(seq_length, dtype=jnp.int32)
    context = attend_heads(query_rot, pair_all, positions, key_pos)
    return context


MESH = pl.DeviceIdType.MESH
plane = 4


def fused_kernel(
    n_line, num_ref, cos_ref, sin_ref, tok_hbm, query_hbm, pair_hbm, out_ref,
    raw, inv_rms, nrm, mine, theirs, wbuf, tok, acc, rsend, rrecv, qrot, kvb, score_buf,
    raw_sem, mine_sem, ck_s, ck_r, w_s, w_r, tl_sem, tp_s, tp_r, ts_s, ts_r,
    rs_s, rs_r, kz_s, kp_s, kb_s, kz_r, ks_r, o_s, o_r,
):
    n_fsdp = n_line * plane
    r = lax.axis_index("rep")
    f = lax.axis_index("fsdp")
    z, p = f // plane, lax.rem(f, plane)
    sib = 1 - r
    n_heads = qrot.shape[0]
    pieces = n_heads + 1
    n_tok = acc.shape[1]
    half = n_tok // 2
    head = acc.shape[2]
    depth = wbuf.shape[2]
    can_up, can_down = z < n_line - 1, z > 0
    to_sib = {"rep": sib}

    def peer(j):
        return lax.rem(p + j, plane)

    def remote(src, dst, send, recv, where):
        return pltpu.make_async_remote_copy(
            src_ref=src, dst_ref=dst, send_sem=send, recv_sem=recv,
            device_id=where, device_id_type=MESH,
        )

    def others(fn, lo=1, hi=n_line):
        for d in range(lo, hi):
            pl.when(z >= d)(functools.partial(fn, z - d, True))
            pl.when(z + d < n_line)(functools.partial(fn, z + d, False))

    raw_copy = pltpu.make_async_copy(
        tok_hbm.at[pl.ds(pl.multiple_of(r * half, half), half), :], raw, raw_sem
    )

    def columns(k, side):
        if k == 0:
            return pair_hbm.at[0, :, pl.ds(pl.multiple_of(side * head, head), head)]
        first = pl.multiple_of((side * n_heads + (k - 1)) * head, head)
        return query_hbm.at[0, :, pl.ds(first, head)]

    def own_ckpt(k):
        return pltpu.make_async_copy(columns(k, r), mine.at[k], mine_sem.at[k])

    def sib_ckpt(k):
        return remote(columns(k, sib), theirs.at[k], ck_s.at[k], ck_r.at[k], to_sib)

    own_ckpt(0).start()
    raw_copy.start()
    for k in range(1, pieces):
        own_ckpt(k).start()

    barrier = pltpu.get_barrier_semaphore()
    pl.semaphore_signal(barrier, inc=1, device_id=to_sib, device_id_type=MESH)
    for j in range(1, plane):
        pl.semaphore_signal(
            barrier, inc=1, device_id={"fsdp": z * plane + peer(j)}, device_id_type=MESH
        )

    @pl.when(can_up)
    def _():
        pl.semaphore_signal(barrier, inc=1, device_id={"fsdp": f + plane}, device_id_type=MESH)

    @pl.when(can_down)
    def _():
        pl.semaphore_signal(barrier, inc=1, device_id={"fsdp": f - plane}, device_id_type=MESH)

    pl.semaphore_wait(barrier, plane + can_up.astype(jnp.int32) + can_down.astype(jnp.int32))

    for k in range(pieces):
        sib_ckpt(k).start()

    def w_copy(k, c, up):
        return remote(
            wbuf.at[k, c], wbuf.at[k, c], w_s.at[k, c, 0 if up else 1], w_r.at[k, c],
            {"fsdp": f + plane if up else f - plane},
        )

    def share(side):
        whole = (num_ref[0] + num_ref[1]).astype(jnp.float32)
        return jnp.full((1, head), num_ref[side].astype(jnp.float32)) / jnp.full((1, head), whole)

    def average(k):
        own_ckpt(k).wait()
        sib_ckpt(k).wait_recv()
        wbuf[k, z] = (share(r) * mine[k] + share(sib) * theirs[k]).astype(jnp.bfloat16)

    def send_own(k):
        pl.when(can_up)(lambda: w_copy(k, z, True).start())
        pl.when(can_down)(lambda: w_copy(k, z, False).start())

    def forward(k, lo=1, hi=n_line):
        def one(c, from_below):
            w_copy(k, c, from_below).wait_recv()
            pl.when(can_up if from_below else can_down)(lambda: w_copy(k, c, from_below).start())

        others(one, lo, hi)

    def near(k):
        forward(k, 1, min(2, n_line))

    def middle(k):
        forward(k, 2, n_line - 1)

    def far(k):
        forward(k, max(2, n_line - 1), n_line)

    def tok_rows(c, chip, side):
        first = pl.multiple_of(chip * n_tok + side * half, half)
        return tok.at[c, pl.ds(first, half), :]

    def tok_own(c):
        return pltpu.make_async_copy(nrm.at[c * plane + p], tok_rows(c, p, r), tl_sem.at[c])

    def tok_own_sib(c):
        return remote(
            nrm.at[c * plane + p], tok_rows(c, p, r), ts_s.at[c, p], ts_r.at[c, p], to_sib
        )

    def tok_peer(c, j):
        q = peer(j)
        return remote(
            nrm.at[c * plane + q], tok_rows(c, p, r), tp_s.at[c, q], tp_r.at[c, p],
            {"fsdp": z * plane + q},
        )

    def tok_arrival(c, j):
        q = peer(j)
        return remote(tok_rows(c, q, r), tok_rows(c, q, r), tp_s.at[c, q], tp_r.at[c, q], to_sib)

    def tok_pass(c, j):
        q = peer(j)
        return remote(tok_rows(c, q, r), tok_rows(c, q, r), ts_s.at[c, q], ts_r.at[c, q], to_sib)

    def tok_from_sib(c, q):
        return remote(
            tok_rows(c, q, sib), tok_rows(c, q, sib), ts_s.at[c, q], ts_r.at[c, q], to_sib
        )

    def inverse_rms(i, carry):
        rows = pl.ds(pl.multiple_of(i * 16, 16), 16)
        wide = raw[rows, :].astype(jnp.float32)
        inv = lax.rsqrt(jnp.mean(wide * wide, axis=-1, keepdims=True) + eps_norm)
        inv_rms[rows, :] = jnp.broadcast_to(inv, (16, inv_rms.shape[1]))
        return carry

    def norm_send(c):
        def norm_rows(i, carry):
            rows = pl.ds(pl.multiple_of(i * 16, 16), 16)
            inv = inv_rms[rows, :1]
            for b in range(c * plane, (c + 1) * plane):
                part = raw[rows, b * depth : (b + 1) * depth].astype(jnp.float32)
                nrm[b, rows, :] = (part * inv).astype(jnp.bfloat16)
            return carry

        lax.fori_loop(0, half // 16, norm_rows, 0)
        for j in (2, 1, 3):
            tok_peer(c, j).start()
        tok_own(c).start()
        tok_own_sib(c).start()

    def tok_collect(c):
        for j in range(1, plane):
            tok_arrival(c, j).wait_recv()
            tok_pass(c, j).start()

    average(0)
    send_own(0)
    raw_copy.wait()
    lax.fori_loop(0, half // 16, inverse_rms, 0)
    average(1)
    send_own(1)
    norm_send(0)
    near(0)
    for k in range(2, pieces):
        average(k)
        send_own(k)
        if k - 1 < n_line:
            norm_send(k - 1)
    for c in range(pieces - 1, n_line):
        norm_send(c)
    middle(0)
    for k in range(1, pieces):
        near(k)
    for c in range(n_line):
        tok_collect(c)
        if c == 0:
            middle(1)
    for c in range(n_line):
        tok_own(c).wait()
        for q in range(plane):
            tok_from_sib(c, q).wait_recv()

    def rs_copy(k, j):
        q = peer(j)
        return remote(
            rsend.at[k, q], rrecv.at[k, p], rs_s.at[k, q], rs_r.at[k, p],
            {"fsdp": z * plane + q},
        )

    def rs_arrival(k, j):
        q = peer(j)
        return remote(rrecv.at[k, q], rrecv.at[k, q], rs_s.at[k, q], rs_r.at[k, q], to_sib)

    def multiply(k):
        for j in (2, 1, 3, 0):
            q = peer(j)
            rows = pl.ds(pl.multiple_of(q * n_tok, n_tok), n_tok)
            part = jnp.dot(tok[0, rows, :], wbuf[k, 0], preferred_element_type=jnp.float32)
            for c in range(1, n_line):
                part += jnp.dot(tok[c, rows, :], wbuf[k, c], preferred_element_type=jnp.float32)
            if j:
                rsend[k, q] = part.astype(jnp.bfloat16)
                rs_copy(k, j).start()
            else:
                acc[k] = part

    def total(k):
        value = acc[k]
        for j in range(1, plane):
            rs_arrival(k, j).wait_recv()
            value += rrecv[k, peer(j)].astype(jnp.float32)
        return value

    def rotate(value):
        return value * cos_ref[...] + pltpu.roll(value, head // 2, 1) * sin_ref[...]

    def kv_rows(b, side):
        return kvb.at[side, pl.ds(pl.multiple_of(b * n_tok, n_tok), n_tok), :]

    def kv_line(c, up):
        b = c * plane + p
        return remote(
            kv_rows(b, r), kv_rows(b, r), kz_s.at[c, 0 if up else 1], kz_r.at[b],
            {"fsdp": f + plane if up else f - plane},
        )

    def kv_plane(c, j):
        b = c * plane + p
        return remote(
            kv_rows(b, r), kv_rows(b, r), kp_s.at[c, peer(j)], kz_r.at[b],
            {"fsdp": z * plane + peer(j)},
        )

    def kv_sib(b):
        return remote(kv_rows(b, r), kv_rows(b, r), kb_s.at[b], ks_r.at[b], to_sib)

    def kv_from_sib(b):
        return remote(kv_rows(b, sib), kv_rows(b, sib), kb_s.at[b], ks_r.at[b], to_sib)

    def kv_arrival(b):
        return remote(kv_rows(b, r), kv_rows(b, r), kb_s.at[b], kz_r.at[b], to_sib)

    def kv_spread(c):
        for j in range(1, plane):
            kv_plane(c, j).start()
        kv_sib(c * plane + p).start()

    def kv_begin():
        value = total(0)
        value = jnp.where(r == 0, rotate(value), value)
        kvb[r, pl.ds(pl.multiple_of(f * n_tok, n_tok), n_tok), :] = value.astype(jnp.bfloat16)
        pl.when(can_up)(lambda: kv_line(z, True).start())
        pl.when(can_down)(lambda: kv_line(z, False).start())
        kv_spread(z)

    def kv_step(lo, hi):
        def one(c, from_below):
            kv_arrival(c * plane + p).wait_recv()
            pl.when(can_up if from_below else can_down)(lambda: kv_line(c, from_below).start())
            kv_spread(c)

        others(one, lo, hi)

    def kv_end():
        for c in range(n_line):
            for j in range(1, plane):
                b = c * plane + peer(j)
                kv_arrival(b).wait_recv()
                kv_sib(b).start()
        for b in range(n_fsdp):
            kv_from_sib(b).wait_recv()

    pair = 2
    block = 2 * n_tok
    scale = math.log2(math.e) / math.sqrt(head)

    def out_copy(h, side):
        col = pl.ds(pl.multiple_of((side * n_heads + h) * head, head), head)
        return remote(out_ref.at[:, col], out_ref.at[:, col], o_s.at[h], o_r.at[h], to_sib)

    def query(h):
        qrot[h] = rotate(total(h + 1)).astype(jnp.bfloat16)

    def attend(h0):
        q = qrot[h0 : h0 + pair].reshape(pair * n_tok, head)
        last = (f * n_tok) // block

        def lanes(values, op):
            groups = [values[:, g * head : (g + 1) * head] for g in range(block // head)]
            return functools.reduce(op, groups)

        def rows_of(i):
            return pl.ds(pl.multiple_of(i * block, block), block)

        def score(i):
            return lax.dot_general(
                q, kvb[0, rows_of(i), :], (((1,), (1,)), ((), ())),
                preferred_element_type=jnp.float32,
            )

        def scored(i, top):
            scores = score(i)
            score_buf[i] = scores
            return jnp.maximum(top, lanes(scores, jnp.maximum))

        scores = score(last)
        row = lax.rem(lax.broadcasted_iota(jnp.int32, scores.shape, 0), n_tok) + f * n_tok
        col = lax.broadcasted_iota(jnp.int32, scores.shape, 1) + last * block
        scores = jnp.where(col <= row, scores, masked_score)
        score_buf[last] = scores
        top = lax.fori_loop(0, last, scored, lanes(scores, jnp.maximum))
        top = jnp.max(top, axis=1, keepdims=True)

        def weighted(i, carry):
            norm, mixed = carry
            weights = jnp.exp2((score_buf[i] - top) * scale)
            mixed += jnp.dot(
                weights.astype(jnp.bfloat16), kvb[1, rows_of(i), :],
                preferred_element_type=jnp.float32,
            )
            return norm + lanes(weights, jnp.add), mixed

        empty = jnp.zeros((pair * n_tok, head), jnp.float32)
        norm, mixed = lax.fori_loop(0, last + 1, weighted, (empty, empty))
        mixed = (mixed / jnp.sum(norm, axis=1, keepdims=True)).astype(jnp.bfloat16)
        for i in range(pair):
            cols = pl.ds(pl.multiple_of((r * n_heads + h0 + i) * head, head), head)
            out_ref[:, cols] = mixed[i * n_tok : (i + 1) * n_tok, :]
            out_copy(h0 + i, r).start()

    far(0)
    multiply(0)
    far(1)
    multiply(1)
    kv_begin()
    middle(2)
    kv_step(1, min(2, n_line))
    middle(3)
    kv_step(2, n_line - 1)
    middle(4)
    far(2)
    multiply(2)
    kv_step(max(2, n_line - 1), n_line)
    far(3)
    multiply(3)
    query(0)
    query(1)
    kv_end()
    far(4)
    multiply(4)
    attend(0)
    query(2)
    query(3)
    attend(2)

    for k in range(pieces):
        sib_ckpt(k).wait_send()
        pl.when(can_up)(lambda k=k: w_copy(k, z, True).wait_send())
        pl.when(can_down)(lambda k=k: w_copy(k, z, False).wait_send())

        def sent(c, from_below, k=k):
            ok = can_up if from_below else can_down
            pl.when(ok)(lambda: w_copy(k, c, from_below).wait_send())

        others(sent)
        for j in range(1, plane):
            rs_copy(k, j).wait_send()
    for c in range(n_line):
        tok_own_sib(c).wait_send()
        for j in range(1, plane):
            tok_peer(c, j).wait_send()
            tok_pass(c, j).wait_send()
            kv_plane(c, j).wait_send()
    pl.when(can_up)(lambda: kv_line(z, True).wait_send())
    pl.when(can_down)(lambda: kv_line(z, False).wait_send())

    def kv_sent(c, from_below):
        ok = can_up if from_below else can_down
        pl.when(ok)(lambda: kv_line(c, from_below).wait_send())

    others(kv_sent)
    for b in range(n_fsdp):
        kv_sib(b).wait_send()
    for h in range(n_heads):
        out_copy(h, r).wait_send()
        out_copy(h, sib).wait_recv()


def fused_local(tokens, query_ckpt, key_value_ckpt, numerators):
    n_fsdp = lax.axis_size("fsdp")
    n_line = n_fsdp // plane
    n_tok, width = tokens.shape
    depth, query_width = query_ckpt.shape[1:]
    head = key_value_ckpt.shape[2] // 2
    n_heads = query_width // head // 2
    pieces = n_heads + 1
    half = n_tok // 2
    positions = lax.axis_index("fsdp") * n_tok + jnp.arange(n_tok, dtype=jnp.int32)
    inverse_freq = jnp.exp(
        -(jnp.arange(head // 2, dtype=jnp.float32) * (2.0 / head)) * math.log(theta_base)
    )
    angles = positions.astype(jnp.float32)[:, None] * inverse_freq[None, :]
    cosine, sine = jnp.cos(angles), jnp.sin(angles)
    cos_table = jnp.concatenate([cosine, cosine], axis=1)
    sin_table = jnp.concatenate([-sine, sine], axis=1)
    vmem, bf16, f32 = pltpu.VMEM, jnp.bfloat16, jnp.float32
    dma = pltpu.SemaphoreType.DMA
    return pl.pallas_call(
        functools.partial(fused_kernel, n_line),
        out_shape=jax.ShapeDtypeStruct((n_tok, query_width), bf16),
        in_specs=[
            pl.BlockSpec(memory_space=pltpu.SMEM),
            pl.BlockSpec(memory_space=pltpu.VMEM),
            pl.BlockSpec(memory_space=pltpu.VMEM),
            pl.BlockSpec(memory_space=pl.ANY),
            pl.BlockSpec(memory_space=pl.ANY),
            pl.BlockSpec(memory_space=pl.ANY),
        ],
        out_specs=pl.BlockSpec(memory_space=pltpu.VMEM),
        scratch_shapes=[
            vmem((half, width), bf16),
            vmem((half, head), f32),
            vmem((n_fsdp, half, depth), bf16),
            vmem((pieces, depth, head), f32),
            vmem((pieces, depth, head), f32),
            vmem((pieces, n_line, depth, head), bf16),
            vmem((n_line, plane * n_tok, depth), bf16),
            vmem((pieces, n_tok, head), f32),
            vmem((pieces, plane, n_tok, head), bf16),
            vmem((pieces, plane, n_tok, head), bf16),
            vmem((n_heads, n_tok, head), bf16),
            vmem((2, n_fsdp * n_tok, head), bf16),
            vmem((n_fsdp // 2, 2 * n_tok, 2 * n_tok), f32),
            dma,
            dma((pieces,)),
            dma((pieces,)),
            dma((pieces,)),
            dma((pieces, n_line, 2)),
            dma((pieces, n_line)),
            dma((n_line,)),
            dma((n_line, plane)),
            dma((n_line, plane)),
            dma((n_line, plane)),
            dma((n_line, plane)),
            dma((pieces, plane)),
            dma((pieces, plane)),
            dma((n_line, 2)),
            dma((n_line, plane)),
            dma((n_fsdp,)),
            dma((n_fsdp,)),
            dma((n_fsdp,)),
            dma((n_heads,)),
            dma((n_heads,)),
        ],
        compiler_params=pltpu.CompilerParams(
            collective_id=0, has_side_effects=True, vmem_limit_bytes=58 * 1024 * 1024
        ),
        cost_estimate=pl.CostEstimate(
            flops=2 * n_tok * width * query_width, bytes_accessed=8 * depth * query_width,
            transcendentals=n_heads * n_tok * n_tok * n_fsdp,
        ),
    )(numerators, cos_table, sin_table, tokens, query_ckpt, key_value_ckpt)


def solution(mesh):
    in_specs = (P("fsdp", None), P("rep", "fsdp", None), P("rep", "fsdp", None), P())
    out_specs = P("fsdp", None)
    paired = mesh.shape["rep"] == 2 and mesh.shape["fsdp"] % plane == 0
    body = fused_local if paired else local
    return jax.shard_map(body, mesh=mesh, in_specs=in_specs, out_specs=out_specs, check_vma=False)
```

```python
import math

import functools

import jax
import jax.numpy as jnp
from jax import lax
from jax.experimental import pallas as pl
from jax.experimental.pallas import tpu as pltpu
from jax.sharding import PartitionSpec as P

theta_base = 500000.0
eps_norm = 1e-05
masked_score = -1e30


def rms_normed(hidden):
    wide_copy = hidden.astype(jnp.float32)
    return (
        wide_copy * lax.rsqrt(jnp.mean(wide_copy * wide_copy, axis=-1, keepdims=True) + eps_norm)
    ).astype(jnp.bfloat16)


def rotary(values, positions):
    half_size = values.shape[-1] // 2
    inverse_freq = jnp.exp(
        -(jnp.arange(half_size, dtype=jnp.float32) * (2.0 / values.shape[-1]))
        * math.log(theta_base)
    )
    angles = positions.astype(jnp.float32)[:, None] * inverse_freq[None, :]
    cosine_table = jnp.cos(angles)[:, None, :]
    sine_table = jnp.sin(angles)[:, None, :]
    first_half = values[..., :half_size]
    second_half = values[..., half_size:]
    return jnp.concatenate(
        [
            first_half * cosine_table - second_half * sine_table,
            second_half * cosine_table + first_half * sine_table,
        ],
        axis=-1,
    )


def attend_heads(queries, pair_rows, query_pos, key_pos):
    head_size = queries.shape[-1]
    key_rows = pair_rows[:, :head_size]
    value_rows = pair_rows[:, head_size:]
    score_scale = 1.0 / math.sqrt(head_size)
    allowed = key_pos[None, :] <= query_pos[:, None]

    def one_head(query_head):
        scores = jnp.dot(query_head, key_rows.T, preferred_element_type=jnp.float32) * score_scale
        scores = jnp.where(allowed, scores, masked_score)
        row_top = jnp.max(scores, axis=1, keepdims=True)
        weights_exp = jnp.exp(scores - row_top)
        norm_sum = jnp.sum(weights_exp, axis=1, keepdims=True)
        mixed_out = (
            jnp.dot(
                weights_exp.astype(jnp.bfloat16), value_rows, preferred_element_type=jnp.float32
            )
            / norm_sum
        )
        return mixed_out.astype(jnp.bfloat16)

    head_outs = lax.map(one_head, jnp.transpose(queries, (1, 0, 2)))
    return jnp.transpose(head_outs, (1, 0, 2)).reshape(queries.shape[0], -1)


def local(tokens, query_ckpt, key_value_ckpt, numerators):
    fsdp_count = lax.axis_size("fsdp")
    rep_idx = lax.axis_index("rep")
    fsdp_idx = lax.axis_index("fsdp")
    slot_ids = jnp.arange(numerators.shape[0], dtype=jnp.int32)
    weight_sum = jnp.sum(numerators).astype(jnp.float32)
    my_share = (
        jnp.sum(jnp.where(slot_ids == rep_idx, numerators, 0)).astype(jnp.float32) / weight_sum
    )
    query_term = my_share * query_ckpt[0]
    pair_term = my_share * key_value_ckpt[0]
    tok_dev = tokens.shape[0]
    seq_length = tok_dev * fsdp_count
    offset = fsdp_idx * tok_dev
    normed = rms_normed(tokens)
    query_width = query_ckpt.shape[2]
    pair_width = key_value_ckpt.shape[2]
    query_sum, pair_sum = lax.psum((query_term, pair_term), "rep")
    query_rows = query_sum.astype(jnp.bfloat16)
    pair_rows = pair_sum.astype(jnp.bfloat16)
    queries = jnp.dot(
        normed,
        lax.all_gather(query_rows, "fsdp", axis=0, tiled=True),
        preferred_element_type=jnp.float32,
    )
    pair_proj = jnp.dot(
        normed,
        lax.all_gather(pair_rows, "fsdp", axis=0, tiled=True),
        preferred_element_type=jnp.float32,
    )
    positions = (offset + jnp.arange(tok_dev, dtype=jnp.int32)) % seq_length
    head_size = pair_width // 2
    query_rot = rotary(
        queries.reshape(tok_dev, query_width // head_size, head_size), positions
    ).astype(jnp.bfloat16)
    key_rot = rotary(pair_proj[:, None, :head_size], positions)[:, 0, :].astype(jnp.bfloat16)
    pair_local = jnp.concatenate([key_rot, pair_proj[:, head_size:].astype(jnp.bfloat16)], axis=1)
    pair_all = lax.all_gather(pair_local, "fsdp", axis=0, tiled=True)
    key_pos = jnp.arange(seq_length, dtype=jnp.int32)
    context = attend_heads(query_rot, pair_all, positions, key_pos)
    return context


MESH = pl.DeviceIdType.MESH
plane = 4


def fused_kernel(
    n_line, num_ref, cos_ref, sin_ref, tok_hbm, query_hbm, pair_hbm, out_ref,
    raw, inv_rms, nrm, mine, theirs, wbuf, tok, acc, rsend, rrecv, qrot, kvb, score_buf,
    raw_sem, mine_sem, ck_s, ck_r, w_s, w_r, tl_sem, tp_s, tp_r, ts_s, ts_r,
    rs_s, rs_r, kz_s, kp_s, kb_s, kz_r, ks_r, o_s, o_r,
):
    n_fsdp = n_line * plane
    r = lax.axis_index("rep")
    f = lax.axis_index("fsdp")
    z, p = f // plane, lax.rem(f, plane)
    sib = 1 - r
    n_heads = qrot.shape[0]
    pieces = n_heads + 1
    n_tok = acc.shape[1]
    half = n_tok // 2
    head = acc.shape[2]
    depth = wbuf.shape[2]
    can_up, can_down = z < n_line - 1, z > 0
    to_sib = {"rep": sib}

    def peer(j):
        return lax.rem(p + j, plane)

    def remote(src, dst, send, recv, where):
        return pltpu.make_async_remote_copy(
            src_ref=src, dst_ref=dst, send_sem=send, recv_sem=recv,
            device_id=where, device_id_type=MESH,
        )

    def others(fn, lo=1, hi=n_line):
        for d in range(lo, hi):
            pl.when(z >= d)(functools.partial(fn, z - d, True))
            pl.when(z + d < n_line)(functools.partial(fn, z + d, False))

    raw_copy = pltpu.make_async_copy(
        tok_hbm.at[pl.ds(pl.multiple_of(r * half, half), half), :], raw, raw_sem
    )

    def columns(k, side):
        if k == 0:
            return pair_hbm.at[0, :, pl.ds(pl.multiple_of(side * head, head), head)]
        first = pl.multiple_of((side * n_heads + (k - 1)) * head, head)
        return query_hbm.at[0, :, pl.ds(first, head)]

    def own_ckpt(k):
        return pltpu.make_async_copy(columns(k, r), mine.at[k], mine_sem.at[k])

    def sib_ckpt(k):
        return remote(columns(k, sib), theirs.at[k], ck_s.at[k], ck_r.at[k], to_sib)

    own_ckpt(0).start()
    raw_copy.start()
    for k in range(1, pieces):
        own_ckpt(k).start()

    barrier = pltpu.get_barrier_semaphore()
    pl.semaphore_signal(barrier, inc=1, device_id=to_sib, device_id_type=MESH)
    for j in range(1, plane):
        pl.semaphore_signal(
            barrier, inc=1, device_id={"fsdp": z * plane + peer(j)}, device_id_type=MESH
        )

    @pl.when(can_up)
    def _():
        pl.semaphore_signal(barrier, inc=1, device_id={"fsdp": f + plane}, device_id_type=MESH)

    @pl.when(can_down)
    def _():
        pl.semaphore_signal(barrier, inc=1, device_id={"fsdp": f - plane}, device_id_type=MESH)

    pl.semaphore_wait(barrier, plane + can_up.astype(jnp.int32) + can_down.astype(jnp.int32))

    for k in range(pieces):
        sib_ckpt(k).start()

    def w_copy(k, c, up):
        return remote(
            wbuf.at[k, c], wbuf.at[k, c], w_s.at[k, c, 0 if up else 1], w_r.at[k, c],
            {"fsdp": f + plane if up else f - plane},
        )

    def share(side):
        whole = (num_ref[0] + num_ref[1]).astype(jnp.float32)
        return jnp.full((1, head), num_ref[side].astype(jnp.float32)) / jnp.full((1, head), whole)

    def average(k):
        own_ckpt(k).wait()
        sib_ckpt(k).wait_recv()
        wbuf[k, z] = (share(r) * mine[k] + share(sib) * theirs[k]).astype(jnp.bfloat16)

    def send_own(k):
        pl.when(can_up)(lambda: w_copy(k, z, True).start())
        pl.when(can_down)(lambda: w_copy(k, z, False).start())

    def forward(k, lo=1, hi=n_line):
        def one(c, from_below):
            w_copy(k, c, from_below).wait_recv()
            pl.when(can_up if from_below else can_down)(lambda: w_copy(k, c, from_below).start())

        others(one, lo, hi)

    def near(k):
        forward(k, 1, min(2, n_line))

    def middle(k):
        forward(k, 2, n_line - 1)

    def far(k):
        forward(k, max(2, n_line - 1), n_line)

    def tok_rows(c, chip, side):
        first = pl.multiple_of(chip * n_tok + side * half, half)
        return tok.at[c, pl.ds(first, half), :]

    def tok_own(c):
        return pltpu.make_async_copy(nrm.at[c * plane + p], tok_rows(c, p, r), tl_sem.at[c])

    def tok_own_sib(c):
        return remote(
            nrm.at[c * plane + p], tok_rows(c, p, r), ts_s.at[c, p], ts_r.at[c, p], to_sib
        )

    def tok_peer(c, j):
        q = peer(j)
        return remote(
            nrm.at[c * plane + q], tok_rows(c, p, r), tp_s.at[c, q], tp_r.at[c, p],
            {"fsdp": z * plane + q},
        )

    def tok_arrival(c, j):
        q = peer(j)
        return remote(tok_rows(c, q, r), tok_rows(c, q, r), tp_s.at[c, q], tp_r.at[c, q], to_sib)

    def tok_pass(c, j):
        q = peer(j)
        return remote(tok_rows(c, q, r), tok_rows(c, q, r), ts_s.at[c, q], ts_r.at[c, q], to_sib)

    def tok_from_sib(c, q):
        return remote(
            tok_rows(c, q, sib), tok_rows(c, q, sib), ts_s.at[c, q], ts_r.at[c, q], to_sib
        )

    def inverse_rms(i, carry):
        rows = pl.ds(pl.multiple_of(i * 16, 16), 16)
        wide = raw[rows, :].astype(jnp.float32)
        inv = lax.rsqrt(jnp.mean(wide * wide, axis=-1, keepdims=True) + eps_norm)
        inv_rms[rows, :] = jnp.broadcast_to(inv, (16, inv_rms.shape[1]))
        return carry

    def norm_send(c):
        def norm_rows(i, carry):
            rows = pl.ds(pl.multiple_of(i * 16, 16), 16)
            inv = inv_rms[rows, :1]
            for b in range(c * plane, (c + 1) * plane):
                part = raw[rows, b * depth : (b + 1) * depth].astype(jnp.float32)
                nrm[b, rows, :] = (part * inv).astype(jnp.bfloat16)
            return carry

        lax.fori_loop(0, half // 16, norm_rows, 0)
        for j in (2, 1, 3):
            tok_peer(c, j).start()
        tok_own(c).start()
        tok_own_sib(c).start()

    def tok_collect(c):
        for j in range(1, plane):
            tok_arrival(c, j).wait_recv()
            tok_pass(c, j).start()

    average(0)
    send_own(0)
    raw_copy.wait()
    lax.fori_loop(0, half // 16, inverse_rms, 0)
    average(1)
    send_own(1)
    norm_send(0)
    near(0)
    for k in range(2, pieces):
        average(k)
        send_own(k)
        if k - 1 < n_line:
            norm_send(k - 1)
    for c in range(pieces - 1, n_line):
        norm_send(c)
    middle(0)
    for k in range(1, pieces):
        near(k)
    for c in range(n_line):
        tok_collect(c)
        if c < 2:
            middle(c + 1)
    for c in range(n_line):
        tok_own(c).wait()
        for q in range(plane):
            tok_from_sib(c, q).wait_recv()

    def rs_copy(k, j):
        q = peer(j)
        return remote(
            rsend.at[k, q], rrecv.at[k, p], rs_s.at[k, q], rs_r.at[k, p],
            {"fsdp": z * plane + q},
        )

    def rs_arrival(k, j):
        q = peer(j)
        return remote(rrecv.at[k, q], rrecv.at[k, q], rs_s.at[k, q], rs_r.at[k, q], to_sib)

    def multiply(k):
        for j in (2, 1, 3, 0):
            q = peer(j)
            rows = pl.ds(pl.multiple_of(q * n_tok, n_tok), n_tok)
            part = jnp.dot(tok[0, rows, :], wbuf[k, 0], preferred_element_type=jnp.float32)
            for c in range(1, n_line):
                part += jnp.dot(tok[c, rows, :], wbuf[k, c], preferred_element_type=jnp.float32)
            if j:
                rsend[k, q] = part.astype(jnp.bfloat16)
                rs_copy(k, j).start()
            else:
                acc[k] = part

    def total(k):
        value = acc[k]
        for j in range(1, plane):
            rs_arrival(k, j).wait_recv()
            value += rrecv[k, peer(j)].astype(jnp.float32)
        return value

    def rotate(value):
        return value * cos_ref[...] + pltpu.roll(value, head // 2, 1) * sin_ref[...]

    def kv_rows(b, side):
        return kvb.at[side, pl.ds(pl.multiple_of(b * n_tok, n_tok), n_tok), :]

    def kv_line(c, up):
        b = c * plane + p
        return remote(
            kv_rows(b, r), kv_rows(b, r), kz_s.at[c, 0 if up else 1], kz_r.at[b],
            {"fsdp": f + plane if up else f - plane},
        )

    def kv_plane(c, j):
        b = c * plane + p
        return remote(
            kv_rows(b, r), kv_rows(b, r), kp_s.at[c, peer(j)], kz_r.at[b],
            {"fsdp": z * plane + peer(j)},
        )

    def kv_sib(b):
        return remote(kv_rows(b, r), kv_rows(b, r), kb_s.at[b], ks_r.at[b], to_sib)

    def kv_from_sib(b):
        return remote(kv_rows(b, sib), kv_rows(b, sib), kb_s.at[b], ks_r.at[b], to_sib)

    def kv_arrival(b):
        return remote(kv_rows(b, r), kv_rows(b, r), kb_s.at[b], kz_r.at[b], to_sib)

    def kv_spread(c):
        for j in range(1, plane):
            kv_plane(c, j).start()
        kv_sib(c * plane + p).start()

    def kv_begin():
        value = total(0)
        value = jnp.where(r == 0, rotate(value), value)
        kvb[r, pl.ds(pl.multiple_of(f * n_tok, n_tok), n_tok), :] = value.astype(jnp.bfloat16)
        pl.when(can_up)(lambda: kv_line(z, True).start())
        pl.when(can_down)(lambda: kv_line(z, False).start())
        kv_spread(z)

    def kv_step(lo, hi):
        def one(c, from_below):
            kv_arrival(c * plane + p).wait_recv()
            pl.when(can_up if from_below else can_down)(lambda: kv_line(c, from_below).start())
            kv_spread(c)

        others(one, lo, hi)

    def kv_end():
        for c in range(n_line):
            for j in range(1, plane):
                b = c * plane + peer(j)
                kv_arrival(b).wait_recv()
                kv_sib(b).start()
        for b in range(n_fsdp):
            kv_from_sib(b).wait_recv()

    block = 2 * n_tok
    scale = math.log2(math.e) / math.sqrt(head)

    def out_copy(h, side):
        col = pl.ds(pl.multiple_of((side * n_heads + h) * head, head), head)
        return remote(out_ref.at[:, col], out_ref.at[:, col], o_s.at[h], o_r.at[h], to_sib)

    def query(h):
        qrot[h] = rotate(total(h + 1)).astype(jnp.bfloat16)

    def attend(h0, count):
        n_rows = count * n_tok
        q = qrot[h0 : h0 + count].reshape(n_rows, head)
        last = (f * n_tok) // block

        def lanes(values, op):
            groups = [values[:, g * head : (g + 1) * head] for g in range(block // head)]
            return functools.reduce(op, groups)

        def rows_of(i):
            return pl.ds(pl.multiple_of(i * block, block), block)

        def score(i):
            return lax.dot_general(
                q, kvb[0, rows_of(i), :], (((1,), (1,)), ((), ())),
                preferred_element_type=jnp.float32,
            )

        def scored(i, top):
            scores = score(i)
            score_buf[i, :n_rows, :] = scores
            return jnp.maximum(top, lanes(scores, jnp.maximum))

        scores = score(last)
        row = lax.rem(lax.broadcasted_iota(jnp.int32, scores.shape, 0), n_tok) + f * n_tok
        col = lax.broadcasted_iota(jnp.int32, scores.shape, 1) + last * block
        scores = jnp.where(col <= row, scores, masked_score)
        score_buf[last, :n_rows, :] = scores
        top = lax.fori_loop(0, last, scored, lanes(scores, jnp.maximum))
        top = jnp.max(top, axis=1, keepdims=True)

        def weighted(i, carry):
            norm, mixed = carry
            weights = jnp.exp2((score_buf[i, :n_rows, :] - top) * scale)
            mixed += jnp.dot(
                weights.astype(jnp.bfloat16), kvb[1, rows_of(i), :],
                preferred_element_type=jnp.float32,
            )
            return norm + lanes(weights, jnp.add), mixed

        empty = jnp.zeros((n_rows, head), jnp.float32)
        norm, mixed = lax.fori_loop(0, last + 1, weighted, (empty, empty))
        mixed = (mixed / jnp.sum(norm, axis=1, keepdims=True)).astype(jnp.bfloat16)
        for i in range(count):
            cols = pl.ds(pl.multiple_of((r * n_heads + h0 + i) * head, head), head)
            out_ref[:, cols] = mixed[i * n_tok : (i + 1) * n_tok, :]
            out_copy(h0 + i, r).start()

    far(0)
    multiply(0)
    far(1)
    multiply(1)
    kv_begin()
    kv_step(1, min(2, n_line))
    middle(3)
    kv_step(2, n_line - 1)
    middle(4)
    far(2)
    multiply(2)
    kv_step(max(2, n_line - 1), n_line)
    far(3)
    multiply(3)
    query(0)
    query(1)
    kv_end()
    attend(0, 2)
    far(4)
    multiply(4)
    query(2)
    attend(2, 1)
    query(3)
    attend(3, 1)

    for k in range(pieces):
        sib_ckpt(k).wait_send()
        pl.when(can_up)(lambda k=k: w_copy(k, z, True).wait_send())
        pl.when(can_down)(lambda k=k: w_copy(k, z, False).wait_send())

        def sent(c, from_below, k=k):
            ok = can_up if from_below else can_down
            pl.when(ok)(lambda: w_copy(k, c, from_below).wait_send())

        others(sent)
        for j in range(1, plane):
            rs_copy(k, j).wait_send()
    for c in range(n_line):
        tok_own_sib(c).wait_send()
        for j in range(1, plane):
            tok_peer(c, j).wait_send()
            tok_pass(c, j).wait_send()
            kv_plane(c, j).wait_send()
    pl.when(can_up)(lambda: kv_line(z, True).wait_send())
    pl.when(can_down)(lambda: kv_line(z, False).wait_send())

    def kv_sent(c, from_below):
        ok = can_up if from_below else can_down
        pl.when(ok)(lambda: kv_line(c, from_below).wait_send())

    others(kv_sent)
    for b in range(n_fsdp):
        kv_sib(b).wait_send()
    for h in range(n_heads):
        out_copy(h, r).wait_send()
        out_copy(h, sib).wait_recv()


def fused_local(tokens, query_ckpt, key_value_ckpt, numerators):
    n_fsdp = lax.axis_size("fsdp")
    n_line = n_fsdp // plane
    n_tok, width = tokens.shape
    depth, query_width = query_ckpt.shape[1:]
    head = key_value_ckpt.shape[2] // 2
    n_heads = query_width // head // 2
    pieces = n_heads + 1
    half = n_tok // 2
    positions = lax.axis_index("fsdp") * n_tok + jnp.arange(n_tok, dtype=jnp.int32)
    inverse_freq = jnp.exp(
        -(jnp.arange(head // 2, dtype=jnp.float32) * (2.0 / head)) * math.log(theta_base)
    )
    angles = positions.astype(jnp.float32)[:, None] * inverse_freq[None, :]
    cosine, sine = jnp.cos(angles), jnp.sin(angles)
    cos_table = jnp.concatenate([cosine, cosine], axis=1)
    sin_table = jnp.concatenate([-sine, sine], axis=1)
    vmem, bf16, f32 = pltpu.VMEM, jnp.bfloat16, jnp.float32
    dma = pltpu.SemaphoreType.DMA
    return pl.pallas_call(
        functools.partial(fused_kernel, n_line),
        out_shape=jax.ShapeDtypeStruct((n_tok, query_width), bf16),
        in_specs=[
            pl.BlockSpec(memory_space=pltpu.SMEM),
            pl.BlockSpec(memory_space=pltpu.VMEM),
            pl.BlockSpec(memory_space=pltpu.VMEM),
            pl.BlockSpec(memory_space=pl.ANY),
            pl.BlockSpec(memory_space=pl.ANY),
            pl.BlockSpec(memory_space=pl.ANY),
        ],
        out_specs=pl.BlockSpec(memory_space=pltpu.VMEM),
        scratch_shapes=[
            vmem((half, width), bf16),
            vmem((half, head), f32),
            vmem((n_fsdp, half, depth), bf16),
            vmem((pieces, depth, head), f32),
            vmem((pieces, depth, head), f32),
            vmem((pieces, n_line, depth, head), bf16),
            vmem((n_line, plane * n_tok, depth), bf16),
            vmem((pieces, n_tok, head), f32),
            vmem((pieces, plane, n_tok, head), bf16),
            vmem((pieces, plane, n_tok, head), bf16),
            vmem((n_heads, n_tok, head), bf16),
            vmem((2, n_fsdp * n_tok, head), bf16),
            vmem((n_fsdp // 2, 2 * n_tok, 2 * n_tok), f32),
            dma,
            dma((pieces,)),
            dma((pieces,)),
            dma((pieces,)),
            dma((pieces, n_line, 2)),
            dma((pieces, n_line)),
            dma((n_line,)),
            dma((n_line, plane)),
            dma((n_line, plane)),
            dma((n_line, plane)),
            dma((n_line, plane)),
            dma((pieces, plane)),
            dma((pieces, plane)),
            dma((n_line, 2)),
            dma((n_line, plane)),
            dma((n_fsdp,)),
            dma((n_fsdp,)),
            dma((n_fsdp,)),
            dma((n_heads,)),
            dma((n_heads,)),
        ],
        compiler_params=pltpu.CompilerParams(
            collective_id=0, has_side_effects=True, vmem_limit_bytes=58 * 1024 * 1024
        ),
        cost_estimate=pl.CostEstimate(
            flops=2 * n_tok * width * query_width, bytes_accessed=8 * depth * query_width,
            transcendentals=n_heads * n_tok * n_tok * n_fsdp,
        ),
    )(numerators, cos_table, sin_table, tokens, query_ckpt, key_value_ckpt)


def solution(mesh):
    in_specs = (P("fsdp", None), P("rep", "fsdp", None), P("rep", "fsdp", None), P())
    out_specs = P("fsdp", None)
    paired = mesh.shape["rep"] == 2 and mesh.shape["fsdp"] % plane == 0
    body = fused_local if paired else local
    return jax.shard_map(body, mesh=mesh, in_specs=in_specs, out_specs=out_specs, check_vma=False)
```
